32 devices in a mesh: dp: 8 (over z, x), rep: 4 (over y, core).
Axes of the slice: x: 2, y: 2, z: 4, core: 2. Of those that a mesh axis runs over, the one named last changes fastest.
Arguments:
- frames_in: bfloat16 [4, 7168, 1536], P('rep', 'dp')
- lengths: int32 [4, 8, 4], P('rep', 'dp'), may hold values from 1 to 893, as said below
- norm_gain: float32 [1536], replicated, may hold values from 0.5 to 1.5
- norm_bias: float32 [1536], replicated, may hold values from -2 to 2
- w_in: bfloat16 [1536, 3072], P(('dp', 'rep')), may hold values from -0.15625 to 0.15625
- kernel: float32 [31, 1536], replicated, may hold values from -1 to 1
- batch_gain: float32 [1536], replicated, may hold values from 0.5 to 1.5
- batch_bias: float32 [1536], replicated, may hold values from -3 to 3
- w_out: bfloat16 [1536, 1536], P(('dp', 'rep')), may hold values from -0.15625 to 0.15625
Outputs:
- frames_out: bfloat16 [4, 7168, 1536], P('rep', 'dp')
The draws below stay inside these ranges and needn't reach their ends.
Inputs may be any that keep to these rules, and one draw needn't show every extreme that they name: `lengths`: for each rep index, the devices 2k and 2k + 1 of dp hold 1024 frames together, so each rep index holds 512 frames for each of its dp devices; a device holds at most 896 frames, and some device of every rep index holds exactly 896.
All inputs are finite; a program needn't handle non-finite values.
Results may differ from the reference program's by a relative error of at most 0.0038.
Values may be sent and summed in bfloat16 or wider, within the bound.
No kernel may reach another device: no remote copies, remote signals or barrier semaphores. Data moves between devices by JAX's collectives and lax.ppermute only.
A program may use at most 128 MiB of HBM per device.

```python
import jax
import jax.numpy as jnp
from jax import lax

D = 1536
FR_DEV = 512
UPD = 4
KERNEL = 31
CAP = 896
N_DP = 8
N_REP = 4


def draw_frames_in(key, part):
    noise_key, pattern_key = jax.random.split(key, 2)
    holder = jnp.arange(N_DP * CAP, dtype=jnp.int32) // CAP
    ramp = 3.0 * holder.astype(jnp.float32) / (N_DP - 1)
    pattern = jax.random.normal(pattern_key, (D,), jnp.float32)
    noise = jax.random.normal(noise_key, (N_REP, N_DP * CAP, D), jnp.float32)
    values = noise + ramp[None, :, None] * pattern[None, None, :]
    return values.astype(jnp.bfloat16)


def draw_lengths(key, part):
    pair_count = N_DP // 2
    surplus = 3 * FR_DEV // 4
    shift_key, chosen_key, heavy_key, piece_key = jax.random.split(key, 4)
    shifts = jax.random.randint(shift_key, (N_REP, pair_count), 0, surplus + 1, jnp.int32)
    chosen = jax.random.randint(chosen_key, (N_REP, 1), 0, pair_count, jnp.int32)
    shifts = jnp.where(jnp.arange(pair_count, dtype=jnp.int32)[None, :] == chosen, surplus, shifts)
    heavy = jax.random.randint(heavy_key, (N_REP, pair_count), 0, 2, jnp.int32) * 2 - 1
    first_load = FR_DEV + heavy * shifts
    device_load = jnp.stack([first_load, 2 * FR_DEV - first_load], axis=2).reshape(N_REP, N_DP)
    lower = device_load // (2 * UPD)
    upper = device_load // UPD + 1
    pieces = jax.random.randint(piece_key, (N_REP, N_DP, UPD - 1), lower[:, :, None], upper[:, :, None], jnp.int32)
    full_device = (device_load == CAP)[:, :, None]
    pieces = jnp.where(full_device, jnp.ones_like(pieces), pieces)
    remainder = device_load - jnp.sum(pieces, axis=2)
    return jnp.concatenate([pieces, remainder[:, :, None]], axis=2).astype(jnp.int32)


def level_of(stream_key, dims, cuts, low, high):
    level = 1.0
    for dim, parts in cuts:
        heights = jax.random.uniform(jax.random.fold_in(jax.random.fold_in(stream_key, 6), dim), (parts,), jnp.float32, low / len(cuts), high / len(cuts))
        level = level * jnp.repeat(jnp.exp(heights), dims[dim] // parts).reshape((-1,) + (1,) * (len(dims) - 1 - dim))
    return level


def gaussian(own_key, dims, scale, limit, shards=(), kind=jnp.bfloat16):
    drawn = scale * jax.random.normal(own_key, dims, jnp.float32)
    if shards:
        drawn = drawn * level_of(own_key, dims, shards, -0.22, 0.18)
    return jnp.clip(drawn, -limit, limit).astype(kind)


def setup_inputs(seed: int = 0) -> dict:
    splits = jax.random.split(jax.random.key(seed), 10)
    return {
        "frames_in": draw_frames_in(jax.random.fold_in(splits[9], 71), 0),
        "lengths": draw_lengths(jax.random.fold_in(splits[9], 71), 0),
        "norm_gain": jnp.clip(1.0 + 0.1 * jax.random.normal(splits[2], (D,), jnp.float32), 0.5, 1.5),
        "norm_bias": gaussian(splits[3], (D,), 0.3, 2.0, (), jnp.float32),
        "w_in": gaussian(splits[4], (D, 2 * D), D ** -0.5, 0.15625, ((0, 32),)),
        "kernel": gaussian(splits[5], (KERNEL, D), KERNEL ** -0.5, 1.0, (), jnp.float32),
        "batch_gain": jnp.clip(1.0 + 0.1 * jax.random.normal(splits[6], (D,), jnp.float32), 0.5, 1.5),
        "batch_bias": gaussian(splits[7], (D,), 0.5, 3.0, (), jnp.float32),
        "w_out": gaussian(splits[8], (D, D), D ** -0.5, 0.15625, ((0, 32),)),
    }


EPSILON = 1e-05

def layer_norm(frames, norm_gain, norm_bias):
    values = frames.astype(jnp.float32)
    average = lax.optimization_barrier(jnp.mean(values, axis=-1, keepdims=True))
    centred = values - average
    spread = lax.optimization_barrier(jnp.mean(centred * centred, axis=-1, keepdims=True))
    return centred * lax.rsqrt(spread + EPSILON) * norm_gain + norm_bias

def depthwise(gated, labels, kernel):
    half_kernel = kernel.shape[0] // 2
    length_rows = gated.shape[0]
    padded = jnp.pad(gated.astype(jnp.float32), ((half_kernel, half_kernel), (0, 0)))
    padded_labels = jnp.pad(labels, (half_kernel, half_kernel), constant_values=-1)
    summed = jnp.zeros(gated.shape, jnp.float32)
    for offset in range(kernel.shape[0]):
        shared = padded_labels[offset:offset + length_rows] == labels
        contribution = jnp.where(shared[:, None], padded[offset:offset + length_rows], 0.0)
        summed = summed + contribution * kernel[offset]
    return summed

def pack_group(group_lengths):
    device_load = lax.optimization_barrier(jnp.sum(group_lengths, axis=1)).astype(jnp.int32)
    offsets = (jnp.cumsum(device_load) - device_load).astype(jnp.int32)
    packed = jnp.arange(N_DP * FR_DEV, dtype=jnp.int32)
    holder = lax.optimization_barrier(jnp.sum((packed[:, None] >= offsets[None, 1:]).astype(jnp.int32), axis=1)).astype(jnp.int32)
    within = (packed - offsets[holder]).astype(jnp.int32)
    source = (holder * CAP + within).astype(jnp.int32)
    boundary = jnp.cumsum(group_lengths, axis=1).astype(jnp.int32)
    utterance = holder * UPD + lax.optimization_barrier(jnp.sum((within[:, None] >= boundary[holder]).astype(jnp.int32), axis=1)).astype(jnp.int32)
    return (source, utterance.astype(jnp.int32))

def reference(frames_in, lengths, norm_gain, norm_bias, w_in, kernel, batch_gain, batch_bias, w_out):

    def first_pass(operands):
        block_frames, group_lengths = operands
        source, utterance = pack_group(group_lengths)
        packed = block_frames[source]
        normed = layer_norm(packed, norm_gain, norm_bias).astype(jnp.bfloat16)
        projected = jnp.dot(normed, w_in, preferred_element_type=jnp.float32)
        gated = (projected[:, :D] * jax.nn.sigmoid(projected[:, D:])).astype(jnp.bfloat16)
        return depthwise(gated, utterance, kernel)
    convolved = lax.map(first_pass, (frames_in, lengths))
    total_count = N_REP * N_DP * FR_DEV
    average = lax.optimization_barrier(jnp.sum(convolved, axis=(0, 1))) / total_count
    spread = lax.optimization_barrier(jnp.sum(jnp.square(convolved - average), axis=(0, 1))) / total_count

    def second_pass(operands):
        block_frames, group_lengths, group_conv = operands
        source, utterance = pack_group(group_lengths)
        scaled = (group_conv - average) * lax.rsqrt(spread + EPSILON) * batch_gain + batch_bias
        active = jax.nn.silu(scaled).astype(jnp.bfloat16)
        branch = jnp.dot(active, w_out, preferred_element_type=jnp.float32)
        mixed = (block_frames[source].astype(jnp.float32) + branch).astype(jnp.bfloat16)
        return jnp.zeros((N_DP * CAP, D), jnp.bfloat16).at[source].set(mixed)
    return lax.map(second_pass, (frames_in, lengths, convolved))
```

```python
import functools

import jax
import jax.numpy as jnp
import numpy as np
from jax import lax
from jax.experimental import pallas as pl
from jax.experimental.pallas import tpu as pltpu
from jax.sharding import PartitionSpec as P

FR_DEV = 512
EPSILON = 1e-05
AXES = ("dp", "rep")
GAP = 16
LANES = 128
VMEM_LIMIT = 48 * 1024 * 1024


def round_up(value, step):
    return -(-value // step) * step


class Grid:
    def __init__(self, n_dp, n_rep):
        self.n_dp, self.n_rep = n_dp, n_rep
        self.x = 2 if n_dp % 2 == 0 else 1
        self.z = n_dp // self.x
        self.c = 2 if n_rep % 2 == 0 else 1
        self.y = n_rep // self.c
        self.count = n_dp * n_rep

    def pairs(self, target):
        found = []
        for d in range(self.n_dp):
            for r in range(self.n_rep):
                z, x = divmod(d, self.x)
                y, c = divmod(r, self.c)
                tz, tx, ty, tc = target(z, x, y, c)
                found.append((d * self.n_rep + r, (tz * self.x + tx) * self.n_rep + ty * self.c + tc))
        return found


class Held:
    def __init__(self, value, owners):
        self.value, self.owners = value, owners

    def sent(self, pairs):
        owners = [None] * len(self.owners)
        for source, target in pairs:
            owners[target] = self.owners[source]
        return Held(lax.ppermute(self.value, AXES, pairs), owners)


def joined(*parts):
    owners = [sum((list(p.owners[i]) for p in parts), []) for i in range(len(parts[0].owners))]
    return Held(jnp.concatenate([p.value for p in parts], axis=0), owners)


def z_ring(grid, held):
    step = grid.pairs(lambda z, x, y, c: ((z + 1) % grid.z, x, y, c))
    parts = [held]
    for _ in range(grid.z - 1):
        parts.append(parts[-1].sent(step))
    return joined(*parts)


def xy_swap(grid, held):
    first = grid.pairs(lambda z, x, y, c: (z, x ^ 1, y, c) if c == 0 else (z, x, y ^ 1, c))
    second = grid.pairs(lambda z, x, y, c: (z, x, y ^ 1, c) if c == 0 else (z, x ^ 1, y, c))
    held = joined(held, held.sent(first))
    return joined(held, held.sent(second))


def gather(grid, shard, z_first):
    held = Held(shard, [[i] for i in range(grid.count)])
    if z_first:
        held = xy_swap(grid, z_ring(grid, held))
    else:
        held = z_ring(grid, xy_swap(grid, held))
    other = held.sent(grid.pairs(lambda z, x, y, c: (z, x, y, c ^ 1)))
    return (held, other)


def place_of(pieces, me):
    table = np.concatenate([np.asarray(p.owners, np.int32) for p in pieces], axis=1)
    return jnp.asarray(table)[me]


def row_bounds(lengths_ref, utterances):
    bounds, total = [0], 0
    for u in range(utterances):
        total = total + lengths_ref[u]
        bounds.append(total)
    return bounds


def norm_kernel(lengths_ref, frames_ref, gain_ref, bias_ref, out_ref, mask_ref, scratch, *, utterances):
    rows = frames_ref.shape[0]
    bounds = row_bounds(lengths_ref, utterances)
    lead = (utterances - 1) * GAP
    width = frames_ref.shape[1]
    scratch[0:lead, :] = jnp.zeros((lead, width), scratch.dtype)
    tail = scratch.shape[0] - lead - rows
    scratch[lead + rows : lead + rows + tail, :] = jnp.zeros((tail, width), scratch.dtype)
    step = 32
    assert rows % step == 0

    @pl.loop(0, rows // step)
    def _(i):
        start = pl.multiple_of(i * step, step)
        values = frames_ref[pl.ds(start, step), :].astype(jnp.float32)
        average = jnp.mean(values, axis=-1, keepdims=True)
        centred = values - average
        spread = jnp.mean(centred * centred, axis=-1, keepdims=True)
        normed = centred * lax.rsqrt(spread + EPSILON) * gain_ref[...] + bias_ref[...]
        scratch[pl.ds(lead + start, step), :] = normed.astype(scratch.dtype)

    @pl.loop(0, out_ref.shape[0] // GAP)
    def _(i):
        start = pl.multiple_of(i * GAP, GAP)
        placed = jnp.zeros((GAP, width), jnp.float32)
        live = jnp.zeros((GAP, LANES), jnp.float32)
        for u in range(utterances):
            row = lax.broadcasted_iota(jnp.int32, (GAP, LANES), 0) + (start - u * GAP)
            inside = (row >= bounds[u]) & (row < bounds[u + 1])
            live = jnp.where(inside, 1.0, live)
            wide = jnp.broadcast_to(inside[:, :1], (GAP, width))
            block = scratch[pl.ds(pl.multiple_of(lead + start - u * GAP, GAP), GAP), :]
            placed = jnp.where(wide, block.astype(jnp.float32), placed)
        out_ref[pl.ds(start, GAP), :] = placed.astype(out_ref.dtype)
        mask_ref[pl.ds(start, GAP), :] = live


def sigmoid(value):
    return 0.5 * jnp.tanh(0.5 * value) + 0.5


def reorder(places_ref, pieces, target):
    shard = sum(p.shape[0] for p in pieces) // places_ref.shape[0]
    at = 0
    for piece in pieces:
        for i in range(piece.shape[0] // shard):
            to = pl.multiple_of(places_ref[at] * shard, 16)
            target[pl.ds(to, shard), :] = piece[i * shard : (i + 1) * shard, :]
            at += 1


def chunk_kernel(*refs, n_pieces, row_tile, halo):
    places_ref, count_ref, normed_ref, mask_ref, taps_ref = refs[:5]
    pieces = refs[5 : 5 + n_pieces]
    conv_ref, stats_ref, weights, gated = refs[5 + n_pieces :]
    rows, depth = normed_ref.shape
    channels = weights.shape[1] // 2
    groups = channels // LANES
    n_taps = taps_ref.shape[0]
    half = n_taps // 2
    reorder(places_ref, pieces, weights)
    for g in range(groups):
        gated[g, 0:halo, :] = jnp.zeros((halo, LANES), jnp.float32)
        gated[g, halo + rows : halo + rows + halo, :] = jnp.zeros((halo, LANES), jnp.float32)

    @pl.loop(0, rows // row_tile)
    def _(i):
        start = pl.multiple_of(i * row_tile, row_tile)
        x = normed_ref[pl.ds(start, row_tile), :]
        for n in range(0, channels, 256):
            value = jnp.dot(x, weights[:, n : n + 256], preferred_element_type=jnp.float32)
            gate = jnp.dot(x, weights[:, channels + n : channels + n + 256], preferred_element_type=jnp.float32)
            product = (value * sigmoid(gate)).astype(jnp.bfloat16).astype(jnp.float32)
            for g in range(2):
                gated[n // LANES + g, pl.ds(halo + start, row_tile), :] = product[:, g * LANES : (g + 1) * LANES]

    block = 64
    for g in range(groups):
        lanes = slice(g * LANES, (g + 1) * LANES)

        def body(i, total):
            start = pl.multiple_of(i * block, block)
            summed = jnp.zeros((block, LANES), jnp.float32)
            for o in range(n_taps):
                summed = summed + gated[g, pl.ds(start + (halo - half + o), block), :] * taps_ref[o : o + 1, lanes]
            conv_ref[pl.ds(start, block), lanes] = summed
            kept = summed * mask_ref[pl.ds(start, block), :]
            return total + jnp.sum(kept.reshape(block // 8, 8, LANES), axis=0)

        total = lax.fori_loop(0, rows // block, body, jnp.zeros((8, LANES), jnp.float32))
        average = jnp.sum(total, axis=0, keepdims=True) / count_ref[0]

        def body2(i, total):
            start = pl.multiple_of(i * block, block)
            centred = (conv_ref[pl.ds(start, block), lanes] - average) * mask_ref[pl.ds(start, block), :]
            return total + jnp.sum((centred * centred).reshape(block // 8, 8, LANES), axis=0)

        total = lax.fori_loop(0, rows // block, body2, jnp.zeros((8, LANES), jnp.float32))
        stats_ref[0:1, lanes] = average
        stats_ref[1:2, lanes] = jnp.sum(total, axis=0, keepdims=True)


def out_kernel(*refs, n_conv, n_pieces, utterances, row_tile):
    places_ref, lengths_ref, frames_ref, average_ref, scale_ref, shift_ref = refs[:6]
    convs = refs[6 : 6 + n_conv]
    pieces = refs[6 + n_conv : 6 + n_conv + n_pieces]
    out_ref, weights, active = refs[6 + n_conv + n_pieces :]
    rows, features = frames_ref.shape
    bounds = row_bounds(lengths_ref, utterances)
    reorder(places_ref, pieces, weights)

    @pl.loop(0, rows // row_tile)
    def _(i):
        start = pl.multiple_of(i * row_tile, row_tile)
        for k in range(row_tile // GAP):
            first = pl.multiple_of(start + k * GAP, GAP)
            row = lax.broadcasted_iota(jnp.int32, (GAP, 1), 0) + first
            at = 0
            for conv in convs:
                width = conv.shape[1]
                values = conv[pl.ds(first, GAP), :]
                for u in range(1, utterances):
                    moved = conv[pl.ds(pl.multiple_of(first + u * GAP, GAP), GAP), :]
                    values = jnp.where(row >= bounds[u], moved, values)
                lanes = slice(at, at + width)
                scaled = (values - average_ref[0:1, lanes]) * scale_ref[0:1, lanes] + shift_ref[0:1, lanes]
                active[k * GAP : (k + 1) * GAP, lanes] = (scaled * sigmoid(scaled)).astype(active.dtype)
                at += width
        row = lax.broadcasted_iota(jnp.int32, (row_tile, 1), 0) + start
        live = row < bounds[utterances]
        for n in range(0, features, 512):
            branch = jnp.dot(active[...], weights[:, n : n + 512], preferred_element_type=jnp.float32)
            mixed = frames_ref[pl.ds(start, row_tile), n : n + 512].astype(jnp.float32) + branch
            out_ref[pl.ds(start, row_tile), n : n + 512] = jnp.where(live, mixed, 0.0).astype(out_ref.dtype)


SMEM = pl.BlockSpec(memory_space=pltpu.SMEM)
VMEM = pl.BlockSpec(memory_space=pltpu.VMEM)
PARAMS = pltpu.CompilerParams(vmem_limit_bytes=VMEM_LIMIT)


def normalise(frames, lengths, gain, bias, padded_rows):
    utterances = lengths.shape[0]
    rows, features = frames.shape
    lead = (utterances - 1) * GAP
    return pl.pallas_call(
        functools.partial(norm_kernel, utterances=utterances),
        out_shape=(
            jax.ShapeDtypeStruct((padded_rows, features), jnp.bfloat16),
            jax.ShapeDtypeStruct((padded_rows, LANES), jnp.float32),
        ),
        in_specs=[SMEM, VMEM, VMEM, VMEM],
        out_specs=(VMEM, VMEM),
        scratch_shapes=[pltpu.VMEM((lead + padded_rows, features), jnp.bfloat16)],
        compiler_params=PARAMS,
        name="normalise",
    )(lengths, frames, gain[None], bias[None])


def chunk(places, count, normed, mask, taps, pieces):
    rows, depth = normed.shape
    channels = pieces[0].shape[1] // 2
    halo = 16
    flops = 2 * rows * depth * channels * 2
    return pl.pallas_call(
        functools.partial(chunk_kernel, n_pieces=len(pieces), row_tile=rows // 3, halo=halo),
        out_shape=(
            jax.ShapeDtypeStruct((rows, channels), jnp.float32),
            jax.ShapeDtypeStruct((2, channels), jnp.float32),
        ),
        in_specs=[SMEM, SMEM] + [VMEM] * (3 + len(pieces)),
        out_specs=(VMEM, VMEM),
        scratch_shapes=[
            pltpu.VMEM((depth, 2 * channels), jnp.bfloat16),
            pltpu.VMEM((channels // LANES, rows + 2 * halo, LANES), jnp.float32),
        ],
        compiler_params=PARAMS,
        cost_estimate=pl.CostEstimate(flops=4 * flops, bytes_accessed=4 * rows * channels, transcendentals=0),
        name="chunk",
    )(places, count, normed, mask, taps, *pieces)


def finish(places, lengths, frames, average, scale, shift, convs, pieces):
    rows, features = frames.shape
    row_tile = 128 if rows % 128 == 0 else GAP
    return pl.pallas_call(
        functools.partial(
            out_kernel,
            n_conv=len(convs),
            n_pieces=len(pieces),
            utterances=lengths.shape[0],
            row_tile=row_tile,
        ),
        out_shape=jax.ShapeDtypeStruct((rows, features), jnp.bfloat16),
        in_specs=[SMEM, SMEM] + [VMEM] * (4 + len(convs) + len(pieces)),
        out_specs=VMEM,
        scratch_shapes=[
            pltpu.VMEM((features, features), jnp.bfloat16),
            pltpu.VMEM((row_tile, features), jnp.bfloat16),
        ],
        compiler_params=PARAMS,
        name="finish",
    )(places, lengths, frames, average, scale, shift, *convs, *pieces)


def merged_stats(grid, count, average, deviation):
    held = jnp.concatenate([average, deviation, jnp.broadcast_to(count, average.shape)], axis=0)
    steps = []
    if grid.c == 2:
        steps.append(lambda z, x, y, c: (z, x, y, c ^ 1))
    for size, move in (
        (grid.x, lambda b: lambda z, x, y, c: (z, x ^ b, y, c)),
        (grid.y, lambda b: lambda z, x, y, c: (z, x, y ^ b, c)),
        (grid.z, lambda b: lambda z, x, y, c: (z ^ b, x, y, c)),
    ):
        bit = 1
        while bit < size:
            steps.append(move(bit))
            bit *= 2
    for step in steps:
        other = lax.ppermute(held, AXES, grid.pairs(step))
        total = held[2:3] + other[2:3]
        delta = other[0:1] - held[0:1]
        share = other[2:3] / total
        held = jnp.concatenate(
            [
                held[0:1] + delta * share,
                held[1:2] + other[1:2] + delta * delta * held[2:3] * share,
                total,
            ],
            axis=0,
        )
    return held[0:1], held[1:2]


def on_device(grid, frames_in, lengths, norm_gain, norm_bias, w_in, kernel, batch_gain, batch_bias, w_out):
    frames = frames_in[0]
    lengths = lengths[0, 0]
    capacity, features = frames.shape
    utterances = lengths.shape[0]
    total_count = grid.count * FR_DEV
    me = lax.axis_index(AXES)
    padded_rows = round_up(capacity + GAP * (utterances - 1), 192)
    part = features // 3
    parts = range(0, features, part)
    shards = [jnp.concatenate([w_in[:, at : at + part], w_in[:, features + at : features + at + part]], axis=1) for at in parts]
    if w_in.shape[0] % 16 == 0:
        held = [gather(grid, shard, True) for shard in shards]
        held_out = gather(grid, w_out, False)
        in_places = place_of(held[0], me)
        out_places = place_of(held_out, me)
        gathered = [[h.value for h in pieces] for pieces in held]
        gathered_out = [h.value for h in held_out]
    else:
        gathered = [[lax.all_gather(shard, AXES, axis=0, tiled=True)] for shard in shards]
        gathered_out = [lax.all_gather(w_out, AXES, axis=0, tiled=True)]
        in_places = out_places = jnp.zeros((1,), jnp.int32)
    normed, mask = normalise(frames, lengths, norm_gain, norm_bias, padded_rows)
    count = jnp.sum(lengths).astype(jnp.float32)
    convs, stats = [], []
    for at, pieces in zip(parts, gathered):
        conv, stat = chunk(in_places, count[None], normed, mask, kernel[:, at : at + part], pieces)
        convs.append(conv)
        stats.append(stat)
    stats = jnp.concatenate(stats, axis=1)
    average, deviation = merged_stats(grid, count, stats[0:1], stats[1:2])
    spread = deviation / total_count
    scale = lax.rsqrt(spread + EPSILON) * batch_gain[None]
    result = finish(out_places, lengths, frames, average, scale, batch_bias[None], convs, gathered_out)
    return result[None]


def solution(mesh):
    grid = Grid(mesh.shape["dp"], mesh.shape["rep"])
    placed = (
        P("rep", "dp", None),
        P("rep", "dp", None),
        P(),
        P(),
        P(("dp", "rep"), None),
        P(),
        P(),
        P(),
        P(("dp", "rep"), None),
    )
    return jax.shard_map(
        functools.partial(on_device, grid),
        mesh=mesh,
        in_specs=placed,
        out_specs=P("rep", "dp", None),
        check_vma=False,
    )
```
